32 devices in a mesh: blk: 8 (over y, x, core), col: 4 (over z).
Axes of the slice: x: 2, y: 2, z: 4, core: 2. Of those that a mesh axis runs over, the one named last changes fastest.
Arguments:
- src_feat: bfloat16 [16, 1024, 256], P('blk', 'col'), may hold values from -40 to 40
- tgt_feat: bfloat16 [16, 1024, 256], P('blk', 'col'), may hold values from -40 to 40
- src_mass: bfloat16 [16, 1024], P('blk', 'col'), may hold values from 0.5 to 2
- tgt_mass: bfloat16 [16, 1024], P('blk', 'col'), may hold values from 0.5 to 2
- candidates: int32 [16, 8], P('blk'), may hold values from 0 to 15, as said below
- counts: int32 [16], P('blk'), may hold values from 1 to 8, as said below
- tgt_home: int32 [16], replicated, may hold values from 0 to 15, each once
Outputs:
- src_aligned: bfloat16 [16, 1024, 256], P('blk', 'col')
- tgt_aligned: bfloat16 [16, 1024, 256], P('blk', 'col')
The draws below stay inside these ranges and needn't reach their ends.
Inputs may be any that keep to these rules, and one draw needn't show every extreme that they name: `candidates`: each row's 8 entries are distinct; the first counts[i] of row i are live, the others are not used; every target block number is among the live entries of some row. `counts`: the 2 blocks of one index of blk hold at most 12 live slots together, and the blocks of some index hold exactly 12. A permutation: target block number j is stored as block tgt_home[j] of tgt_feat and tgt_mass.
All inputs are finite; a program needn't handle non-finite values.
Results may differ from the reference program's by a relative error of at most 0.017.
Values may be sent and summed in bfloat16 or wider, within the bound.
A program may use at most 64 MiB of HBM per device.

```python
import math
import jax
import jax.numpy as jnp
from jax import lax

W = 256
B = 1024
KMAX = 8
ITERS = 2
BPD = 2
NB = 16


def feature_draw(key):
    key_one, key_two, key_three = jax.random.split(key, 3)
    row_scales = jnp.exp(jax.random.uniform(key_one, (NB, B, 1), jnp.float32, math.log(0.3), math.log(3.0)))
    col_scales = jnp.exp(jax.random.uniform(key_two, (1, 1, W), jnp.float32, math.log(0.3), math.log(3.0)))
    values = jax.random.normal(key_three, (NB, B, W), jnp.float32) * row_scales * col_scales
    return jnp.clip(values, -40.0, 40.0).astype(jnp.bfloat16)


def draw_src_feat(key, part):
    return feature_draw(jax.random.fold_in(key, 31))


def draw_tgt_feat(key, part):
    return feature_draw(jax.random.fold_in(key, 37))


def draw_candidates(key, part):
    key_one, key_two = jax.random.split(jax.random.fold_in(key, 11))
    leading = jax.random.permutation(key_one, NB).astype(jnp.int32)
    row_keys = jax.random.split(key_two, NB)
    offsets = jax.vmap(lambda row_key: jax.random.permutation(row_key, NB - 1)[:KMAX - 1] + 1)(row_keys)
    trailing = (leading[:, None] + offsets.astype(jnp.int32)) % NB
    return jnp.concatenate([leading[:, None], trailing], axis=1).astype(jnp.int32)


def draw_counts(key, part):
    key_one, key_two, key_three = jax.random.split(jax.random.fold_in(key, 23), 3)
    first_draw = jax.random.randint(key_one, (NB,), 0, 8)
    second_draw = jax.random.randint(key_two, (NB,), 0, 8)
    typical = 1 + first_draw * second_draw // 12
    loaded = jax.random.randint(key_three, (), 0, NB // BPD)
    position = jnp.arange(NB) % BPD
    forced = jnp.where(position == 0, KMAX, jnp.where(position == BPD - 1, 12 - KMAX, 6))
    in_group = jnp.arange(NB) // BPD == loaded
    return jnp.where(in_group, forced, typical).astype(jnp.int32)


def level_of(key, dims, cuts, smallest, high):
    factor_of = 1.0
    for axis_at, shards_of in cuts:
        heights = jax.random.uniform(jax.random.fold_in(jax.random.fold_in(key, 6), axis_at), (shards_of,), jnp.float32, smallest / len(cuts), high / len(cuts))
        factor_of = factor_of * jnp.repeat(jnp.exp(heights), dims[axis_at] // shards_of).reshape((-1,) + (1,) * (len(dims) - 1 - axis_at))
    return factor_of


def setup_inputs(seed: int = 0) -> dict:
    keys = jax.random.split(jax.random.key(seed), 8)
    src_feat = draw_src_feat(jax.random.fold_in(keys[7], 71), 0)
    tgt_feat = draw_tgt_feat(jax.random.fold_in(keys[7], 71), 0)
    src_mass = jnp.clip(jnp.exp(math.log(2.0) - 1.3862944 * jax.random.uniform(keys[2], (NB, B), jnp.float32) ** level_of(keys[2], (NB, B), ((0, 8), (1, 4)), -0.2, 0.2)), 0.5, 2.0).astype(jnp.bfloat16)
    tgt_mass = jnp.clip(jnp.exp(math.log(2.0) - 1.3862944 * jax.random.uniform(keys[3], (NB, B), jnp.float32) ** level_of(keys[3], (NB, B), ((0, 8), (1, 4)), -0.2, 0.2)), 0.5, 2.0).astype(jnp.bfloat16)
    candidates = draw_candidates(jax.random.fold_in(keys[7], 71), 0)
    counts = draw_counts(jax.random.fold_in(keys[7], 71), 0)
    tgt_home = jax.random.permutation(keys[6], NB).astype(jnp.int32)
    return dict(src_feat=src_feat, tgt_feat=tgt_feat, src_mass=src_mass, tgt_mass=tgt_mass, candidates=candidates, counts=counts, tgt_home=tgt_home)


score_offset = 0.3
softness_level = 0.02
epsilon = 1e-06
highest = lax.Precision.HIGHEST

def unit_rows(features):
    values = features.astype(jnp.float32)
    inverse = lax.rsqrt(lax.optimization_barrier(jnp.mean(values * values, axis=-1, keepdims=True)) + epsilon)
    return (values * inverse).astype(jnp.bfloat16)

def reference(src_feat, tgt_feat, src_mass, tgt_mass, candidates, counts, tgt_home):
    block_count, block_rows, feature_total = src_feat.shape
    slot_max = candidates.shape[1]
    src_unit = unit_rows(src_feat)
    tgt_unit = unit_rows(tgt_feat)
    src_weight = src_mass.astype(jnp.float32)
    tgt_weight = tgt_mass.astype(jnp.float32)
    slot_index = jnp.arange(block_count * slot_max, dtype=jnp.int32)
    src_of = (slot_index // slot_max).astype(jnp.int32)
    tgt_of = jnp.take(tgt_home, candidates.reshape(-1)).astype(jnp.int32)
    alive_flag = slot_index % slot_max < jnp.take(counts, src_of)
    slot_data = (src_of, tgt_of, alive_flag)

    def kernel_of(src_index, tgt_index):
        src_block = lax.dynamic_index_in_dim(src_unit, src_index, 0, keepdims=False)
        tgt_tile = lax.dynamic_index_in_dim(tgt_unit, tgt_index, 0, keepdims=False)
        score_matrix = jnp.dot(src_block, tgt_tile.T, preferred_element_type=jnp.float32)
        return jnp.exp((score_matrix / feature_total - score_offset) / softness_level)

    def row_pass(column_scaling_vector):

        def step(running, entry):
            src_index, tgt_index, alive = entry

            def compute_slot(current):
                kernel_tile = kernel_of(src_index, tgt_index)
                v_rows = lax.dynamic_index_in_dim(column_scaling_vector, tgt_index, 0, keepdims=False)
                row_part = jnp.dot(kernel_tile, v_rows, precision=highest)
                before = lax.dynamic_index_in_dim(current, src_index, 0, keepdims=False)
                return lax.dynamic_update_index_in_dim(current, before + row_part, src_index, 0)
            return (lax.cond(alive, compute_slot, lambda current: current, running), None)
        result, _ = lax.scan(step, jnp.zeros((block_count, block_rows), jnp.float32), slot_data)
        return result

    def col_pass(scaling_u):

        def step(running, entry):
            src_index, tgt_index, alive = entry

            def compute_slot(current):
                kernel_tile = kernel_of(src_index, tgt_index)
                u_rows = lax.dynamic_index_in_dim(scaling_u, src_index, 0, keepdims=False)
                col_part = jnp.dot(u_rows, kernel_tile, precision=highest)
                before = lax.dynamic_index_in_dim(current, tgt_index, 0, keepdims=False)
                return lax.dynamic_update_index_in_dim(current, before + col_part, tgt_index, 0)
            return (lax.cond(alive, compute_slot, lambda current: current, running), None)
        result, _ = lax.scan(step, jnp.zeros((block_count, block_rows), jnp.float32), slot_data)
        return result
    column_scaling_vector = jnp.ones((block_count, block_rows), jnp.float32)
    scaling_u = jnp.ones((block_count, block_rows), jnp.float32)
    for iteration in range(ITERS):
        scaling_u = src_weight / row_pass(column_scaling_vector)
        column_scaling_vector = tgt_weight / col_pass(scaling_u)

    def final_step(running, entry):
        src_index, tgt_index, alive = entry

        def compute_slot(current):
            src_sums, tgt_sums = current
            kernel_tile = kernel_of(src_index, tgt_index)
            u_rows = lax.dynamic_index_in_dim(scaling_u, src_index, 0, keepdims=False)
            v_rows = lax.dynamic_index_in_dim(column_scaling_vector, tgt_index, 0, keepdims=False)
            plan = (u_rows[:, None] * kernel_tile * v_rows[None, :]).astype(jnp.bfloat16)
            tgt_raw = lax.dynamic_index_in_dim(tgt_feat, tgt_index, 0, keepdims=False)
            src_raw = lax.dynamic_index_in_dim(src_feat, src_index, 0, keepdims=False)
            toward = jnp.dot(plan, tgt_raw, preferred_element_type=jnp.float32)
            back_terms = jnp.dot(plan.T, src_raw, preferred_element_type=jnp.float32)
            before_src = lax.dynamic_index_in_dim(src_sums, src_index, 0, keepdims=False)
            before_tgt = lax.dynamic_index_in_dim(tgt_sums, tgt_index, 0, keepdims=False)
            src_sums = lax.dynamic_update_index_in_dim(src_sums, before_src + toward, src_index, 0)
            tgt_sums = lax.dynamic_update_index_in_dim(tgt_sums, before_tgt + back_terms, tgt_index, 0)
            return (src_sums, tgt_sums)
        return (lax.cond(alive, compute_slot, lambda current: current, running), None)
    empty_sums = jnp.zeros((block_count, block_rows, feature_total), jnp.float32)
    (src_sums, tgt_sums), _ = lax.scan(final_step, (empty_sums, empty_sums), slot_data)
    src_aligned = (src_sums / src_weight[:, :, None]).astype(jnp.bfloat16)
    tgt_aligned = (tgt_sums / tgt_weight[:, :, None]).astype(jnp.bfloat16)
    return (src_aligned, tgt_aligned)
```

```python
import functools
import math

import jax
import jax.numpy as jnp
from jax import lax
from jax.experimental import pallas as pl
from jax.experimental.pallas import tpu as pltpu
from jax.sharding import PartitionSpec as P

ITERS = 2
PAIRS = 12
MESH = pl.DeviceIdType.MESH
F32, BF16 = jnp.float32, jnp.bfloat16
LOG2E = math.log2(math.e)
SCALE = LOG2E / 0.02
SHIFT = -0.3 * LOG2E / 0.02
DEAD = -1e30
NT = (((1,), (1,)), ((), ()))


def unit_rows(values):
    inverse = lax.rsqrt(jnp.mean(values * values, axis=-1, keepdims=True) + 1e-6)
    return (values * inverse).astype(BF16)


def split_rows(row):
    wide = jnp.broadcast_to(row, (16, row.shape[1]))
    high = wide.astype(BF16).astype(F32)
    first = lax.broadcasted_iota(jnp.int32, wide.shape, 0) < 8
    return jnp.where(first, high, wide - high).astype(BF16)


def column_of(row, width):
    turned = jnp.transpose(jnp.broadcast_to(row, (128, row.shape[1])))
    return jnp.concatenate([turned] * (width // 128), axis=1)


def kernel(nb_dev, nc, src_ref, tgt_ref, smass_ref, tmass_ref, cand_ref, count_ref, home_ref,
           src_out, tgt_out, src_all, src_unit, src_turned, tgt_all, kmat, smass_all, tmass_all,
           u_rep, v_rep, row_parts, col_parts, row_tot, col_tot, back, acc, src_send, src_recv,
           tgt_send, tgt_recv, slot_src, slot_tgt, slot_bias, pair_slot,
           col_ss, col_rs, blk_ss, blk_rs):
    b, c = lax.axis_index("blk"), lax.axis_index("col")
    local_blocks, sub, width = src_ref.shape
    slot_max = cand_ref.shape[1]
    blocks = tgt_all.shape[0]
    full = src_all.shape[1]

    barrier = pltpu.get_barrier_semaphore()
    for d in range(1, nc):
        pl.semaphore_signal(barrier, inc=1, device_id={"col": lax.rem(c + d, nc)}, device_id_type=MESH)
    for d in range(1, nb_dev):
        pl.semaphore_signal(barrier, inc=1, device_id={"blk": lax.rem(b + d, nb_dev)}, device_id_type=MESH)
    pl.semaphore_wait(barrier, nc + nb_dev - 2)

    def to_col(kind, source, target):
        out = []
        for d in range(1, nc):
            peer = lax.rem(c + d, nc)
            copy = pltpu.make_async_remote_copy(
                src_ref=source(peer), dst_ref=target, send_sem=col_ss.at[kind, d],
                recv_sem=col_rs.at[kind, d], device_id={"col": peer}, device_id_type=MESH)
            copy.start()
            out.append(copy)
        return out

    def to_blk(kind, source, target):
        out = []
        for d in range(1, nb_dev):
            peer = lax.rem(b + d, nb_dev)
            copy = pltpu.make_async_remote_copy(
                src_ref=source(peer), dst_ref=target, send_sem=blk_ss.at[kind, d],
                recv_sem=blk_rs.at[kind, d], device_id={"blk": peer}, device_id_type=MESH)
            copy.start()
            out.append(copy)
        return out

    def finish(copies):
        for copy in copies:
            copy.wait()

    my_rows = pl.ds(pl.multiple_of(c * sub, sub), sub)
    my_blocks = pl.ds(b * local_blocks, local_blocks)
    src_copies = to_col(0, lambda peer: src_ref, src_all.at[:, my_rows, :])
    tgt_copies = to_blk(0, lambda peer: tgt_ref, tgt_all.at[my_blocks])
    mass_copies = to_col(1, lambda peer: smass_ref, smass_all.at[c])
    mass_copies += to_blk(1, lambda peer: tmass_ref, tmass_all.at[my_blocks])
    src_all[:, my_rows, :] = src_ref[...]
    tgt_all[my_blocks] = tgt_ref[...]
    smass_all[c] = smass_ref[...]
    tmass_all[my_blocks] = tmass_ref[...]

    total = count_ref[0]
    for p in range(1, local_blocks):
        total = total + count_ref[p]
    for s in range(PAIRS):
        owner, start, end = 0, 0, count_ref[0]
        for p in range(1, local_blocks):
            owner = jnp.where(s >= end, p, owner)
            start = jnp.where(s >= end, end, start)
            end = end + count_ref[p]
        within = jnp.minimum(s - start, slot_max - 1)
        alive = s < total
        slot_src[s] = jnp.int32(owner)
        slot_tgt[s] = jnp.where(alive, home_ref[cand_ref[owner, within]], blocks)
        slot_bias[s] = jnp.where(alive, F32(SHIFT), F32(DEAD))

    @pl.loop(0, blocks)
    def _(n):
        for p in range(local_blocks):
            found = jnp.int32(PAIRS)
            for s in range(PAIRS):
                hit = jnp.logical_and(slot_src[s] == p, slot_tgt[s] == n)
                found = jnp.where(hit, s, found)
            pair_slot[n, p] = found

    back[PAIRS] = jnp.zeros(back.shape[1:], F32)
    acc[...] = jnp.zeros(acc.shape, F32)
    finish(src_copies)

    @pl.loop(0, nc)
    def _(piece):
        rows = pl.ds(pl.multiple_of(piece * sub, sub), sub)
        for p in range(local_blocks):
            values = src_all[p, rows, :].astype(F32)
            src_unit[p, rows, :] = unit_rows(values)
            src_turned[p, :, rows] = jnp.transpose(values).astype(BF16)

    finish(tgt_copies)

    row_ids = lax.broadcasted_iota(jnp.int32, (8, full), 0)
    block_ids = lax.broadcasted_iota(jnp.int32, (blocks, sub), 0)
    ones = jnp.where(lax.broadcasted_iota(jnp.int32, (16, sub), 0) < 8, F32(1), F32(0)).astype(BF16)

    def row_part(s, v_rows, running):
        found = lax.dot_general(v_rows, kmat[s], NT, preferred_element_type=F32)
        return running + jnp.where(row_ids == slot_src[s], found[:8] + found[8:], 0.0)

    def first_step(s, running):
        source, target = slot_src[s], jnp.minimum(slot_tgt[s], blocks - 1)
        bias = slot_bias[s]
        tile = unit_rows(tgt_all[target].astype(F32))
        chunk = 256
        for at in range(0, full, chunk):
            score = lax.dot_general(src_unit[source, at:at + chunk, :], tile, NT,
                                    preferred_element_type=F32)
            kmat[s, at:at + chunk, :] = jnp.exp2(score * F32(SCALE / width) + bias).astype(BF16)
        return row_part(s, ones, running)

    def later_step(s, running):
        return row_part(s, v_rep[jnp.minimum(slot_tgt[s], blocks - 1)], running)

    def col_step(s, running):
        found = jnp.dot(u_rep[slot_src[s]], kmat[s], preferred_element_type=F32)
        found = found[:8] + found[8:]
        return running + jnp.where(block_ids == slot_tgt[s], found[:1], 0.0)

    for step in range(ITERS):
        row_parts[step, c] = lax.fori_loop(
            0, PAIRS, first_step if step == 0 else later_step, jnp.zeros((8, full), F32))
        finish(to_col(2 + step, lambda peer: row_parts.at[step, c], row_parts.at[step, c]))
        rows = row_parts[step, 0]
        for at in range(1, nc):
            rows = rows + row_parts[step, at]
        rows = jnp.where(row_ids < local_blocks, rows, 1.0)
        row_tot[...] = rows
        if step == 0:
            finish(mass_copies)
        masses = jnp.concatenate([smass_all[at] for at in range(nc)], axis=1)
        scaling_u = masses / rows
        for p in range(local_blocks):
            u_rep[p] = split_rows(scaling_u[p:p + 1])
            if step == ITERS - 1:
                src_turned[p] = (src_turned[p].astype(F32) * scaling_u[p:p + 1]).astype(BF16)
        col_parts[step, b] = lax.fori_loop(0, PAIRS, col_step, jnp.zeros((blocks, sub), F32))
        col_copies = to_blk(2 + step, lambda peer: col_parts.at[step, b], col_parts.at[step, b])
        if step == ITERS - 1:
            @pl.loop(0, PAIRS)
            def _(s):
                back[s] = jnp.dot(src_turned[slot_src[s]], kmat[s], preferred_element_type=F32)

            @pl.loop(0, blocks)
            def _(n):
                piece = back[pair_slot[n, 0]]
                for p in range(1, local_blocks):
                    piece = piece + back[pair_slot[n, p]]
                tgt_send[n] = piece.astype(BF16)
        finish(col_copies)
        columns = col_parts[step, 0]
        for at in range(1, nb_dev):
            columns = columns + col_parts[step, at]
        col_tot[...] = columns
        if step == ITERS - 1:
            tgt_sums = to_blk(
                2 + ITERS, lambda peer: tgt_send.at[pl.ds(peer * local_blocks, local_blocks)],
                tgt_recv.at[b])

        @pl.loop(0, blocks)
        def _(n):
            row = tmass_all[n, :1, :] / col_tot[pl.ds(n, 1), :]
            if step < ITERS - 1:
                v_rep[n] = split_rows(row)
            else:
                tgt_all[n] = (tgt_all[n].astype(F32) * column_of(row, width)).astype(BF16)

    @pl.loop(0, PAIRS)
    def _(s):
        tile = tgt_all[jnp.minimum(slot_tgt[s], blocks - 1)]
        source = slot_src[s]
        chunk = 256
        for at in range(0, full, chunk):
            toward = jnp.dot(kmat[s, at:at + chunk, :], tile, preferred_element_type=F32)
            for p in range(local_blocks):
                hot = jnp.where(source == p, F32(1), F32(0))
                acc[p, at:at + chunk, :] += toward * hot

    for at in range(nc):
        src_send[at] = acc[:, at * sub:(at + 1) * sub, :].astype(BF16)
    src_sums = to_col(2 + ITERS, lambda peer: src_send.at[peer], src_recv.at[c])
    src_recv[c] = src_send[c]
    tgt_recv[b] = tgt_send[my_blocks]
    finish(src_sums)
    for p in range(local_blocks):
        whole = src_recv[0, p].astype(F32)
        for at in range(1, nc):
            whole = whole + src_recv[at, p].astype(F32)
        src_out[p] = (whole / column_of(row_tot[p:p + 1, my_rows], width)).astype(BF16)
    finish(tgt_sums)
    for q in range(local_blocks):
        whole = tgt_recv[0, q].astype(F32)
        for at in range(1, nb_dev):
            whole = whole + tgt_recv[at, q].astype(F32)
        whole = whole / col_tot[pl.ds(b * local_blocks + q, 1), :]
        tgt_out[q] = jnp.transpose(whole).astype(BF16)


def local(nb_dev, nc, src_feat, tgt_feat, src_mass, tgt_mass, candidates, counts, tgt_home):
    local_blocks, sub, width = src_feat.shape
    blocks = tgt_home.shape[0]
    full = sub * nc
    smass = jnp.pad(src_mass.astype(F32), ((0, 8 - local_blocks), (0, 0)))
    tmass = jnp.broadcast_to(tgt_mass.astype(F32)[:, None, :], (local_blocks, 8, sub))
    vmem = pl.BlockSpec(memory_space=pltpu.VMEM)
    smem = pl.BlockSpec(memory_space=pltpu.SMEM)
    kinds = 3 + ITERS
    shape = jax.ShapeDtypeStruct((local_blocks, sub, width), BF16)
    flops = 2 * PAIRS * full * sub * width * 3
    return pl.pallas_call(
        functools.partial(kernel, nb_dev, nc),
        out_shape=(shape, shape),
        in_specs=[vmem] * 4 + [smem] * 3,
        out_specs=(vmem, vmem),
        scratch_shapes=[
            pltpu.VMEM((local_blocks, full, width), BF16),
            pltpu.VMEM((local_blocks, full, width), BF16),
            pltpu.VMEM((local_blocks, width, full), BF16),
            pltpu.VMEM((blocks, sub, width), BF16),
            pltpu.VMEM((PAIRS, full, sub), BF16),
            pltpu.VMEM((nc, 8, sub), F32),
            pltpu.VMEM((blocks, 8, sub), F32),
            pltpu.VMEM((local_blocks, 16, full), BF16),
            pltpu.VMEM((blocks, 16, sub), BF16),
            pltpu.VMEM((ITERS, nc, 8, full), F32),
            pltpu.VMEM((ITERS, nb_dev, blocks, sub), F32),
            pltpu.VMEM((8, full), F32),
            pltpu.VMEM((blocks, sub), F32),
            pltpu.VMEM((PAIRS + 1, width, sub), F32),
            pltpu.VMEM((local_blocks, full, width), F32),
            pltpu.VMEM((nc, local_blocks, sub, width), BF16),
            pltpu.VMEM((nc, local_blocks, sub, width), BF16),
            pltpu.VMEM((blocks, width, sub), BF16),
            pltpu.VMEM((nb_dev, local_blocks, width, sub), BF16),
            pltpu.SMEM((PAIRS,), jnp.int32),
            pltpu.SMEM((PAIRS,), jnp.int32),
            pltpu.SMEM((PAIRS,), F32),
            pltpu.SMEM((blocks, local_blocks), jnp.int32),
            pltpu.SemaphoreType.DMA((kinds, nc)),
            pltpu.SemaphoreType.DMA((kinds, nc)),
            pltpu.SemaphoreType.DMA((kinds, nb_dev)),
            pltpu.SemaphoreType.DMA((kinds, nb_dev)),
        ],
        compiler_params=pltpu.CompilerParams(
            collective_id=0, has_side_effects=True, vmem_limit_bytes=56 * 1024 * 1024),
        cost_estimate=pl.CostEstimate(
            flops=flops, bytes_accessed=4 * local_blocks * sub * width * 2,
            transcendentals=PAIRS * full * sub),
    )(src_feat, tgt_feat, smass, tmass, candidates, counts, tgt_home)


def solution(mesh):
    in_specs = (
        P("blk", "col", None),
        P("blk", "col", None),
        P("blk", "col"),
        P("blk", "col"),
        P("blk", None),
        P("blk"),
        P(),
    )
    out_specs = (P("blk", "col", None), P("blk", "col", None))
    return jax.shard_map(
        functools.partial(local, mesh.shape["blk"], mesh.shape["col"]),
        mesh=mesh, in_specs=in_specs, out_specs=out_specs, check_vma=False)
```

```python
import functools
import math

import jax
import jax.numpy as jnp
from jax import lax
from jax.experimental import pallas as pl
from jax.experimental.pallas import tpu as pltpu
from jax.sharding import PartitionSpec as P

ITERS = 2
PAIRS = 12
MESH = pl.DeviceIdType.MESH
F32, BF16 = jnp.float32, jnp.bfloat16
LOG2E = math.log2(math.e)
SCALE = LOG2E / 0.02
SHIFT = -0.3 * LOG2E / 0.02
DEAD = -1e30
NT = (((1,), (1,)), ((), ()))


def unit_rows(values):
    inverse = lax.rsqrt(jnp.mean(values * values, axis=-1, keepdims=True) + 1e-6)
    return (values * inverse).astype(BF16)


def split_rows(row):
    wide = jnp.broadcast_to(row, (16, row.shape[1]))
    high = wide.astype(BF16).astype(F32)
    first = lax.broadcasted_iota(jnp.int32, wide.shape, 0) < 8
    return jnp.where(first, high, wide - high).astype(BF16)


def column_of(row, width):
    turned = jnp.transpose(jnp.broadcast_to(row, (128, row.shape[1])))
    return jnp.concatenate([turned] * (width // 128), axis=1)


def kernel(nb_dev, nc, src_ref, tgt_ref, smass_ref, tmass_ref, cand_ref, count_ref, home_ref,
           src_out, tgt_out, src_all, src_unit, src_turned, tgt_all, kmat, smass_all, tmass_all,
           u_rep, v_rep, row_parts, col_parts, row_tot, col_tot, back, acc, src_send, src_recv,
           tgt_send, tgt_recv, pair_send, pair_recv, tile_unit, slot_src, slot_tgt, slot_bias, pair_slot,
           col_ss, col_rs, blk_ss, blk_rs):
    b, c = lax.axis_index("blk"), lax.axis_index("col")
    local_blocks, sub, width = src_ref.shape
    slot_max = cand_ref.shape[1]
    blocks = tgt_all.shape[0]
    full = src_all.shape[1]

    barrier = pltpu.get_barrier_semaphore()
    for d in range(1, nc):
        pl.semaphore_signal(barrier, inc=1, device_id={"col": lax.rem(c + d, nc)}, device_id_type=MESH)
    for d in range(1, nb_dev):
        pl.semaphore_signal(barrier, inc=1, device_id={"blk": lax.rem(b + d, nb_dev)}, device_id_type=MESH)
    pl.semaphore_wait(barrier, nc + nb_dev - 2)

    def to_col(kind, source, target):
        out = []
        for d in range(1, nc):
            peer = lax.rem(c + d, nc)
            copy = pltpu.make_async_remote_copy(
                src_ref=source(peer), dst_ref=target, send_sem=col_ss.at[kind, d],
                recv_sem=col_rs.at[kind, d], device_id={"col": peer}, device_id_type=MESH)
            copy.start()
            out.append(copy)
        return out

    mate = b + 1 - 2 * lax.rem(b, 2)

    def blk_copy(kind, d, peer, source, target):
        copy = pltpu.make_async_remote_copy(
            src_ref=source, dst_ref=target, send_sem=blk_ss.at[kind, d],
            recv_sem=blk_rs.at[kind, d], device_id={"blk": peer}, device_id_type=MESH)
        copy.start()
        return copy

    def blocks_of(index):
        return pl.ds(index * local_blocks, local_blocks)

    def to_blk(kind, source, target):
        out = []
        for d in range(1, nb_dev):
            peer = lax.rem(b + d, nb_dev)
            copy = pltpu.make_async_remote_copy(
                src_ref=source(peer), dst_ref=target, send_sem=blk_ss.at[kind, d],
                recv_sem=blk_rs.at[kind, d], device_id={"blk": peer}, device_id_type=MESH)
            copy.start()
            out.append(copy)
        return out

    def finish(copies):
        for copy in copies:
            copy.wait()

    my_rows = pl.ds(pl.multiple_of(c * sub, sub), sub)
    my_blocks = pl.ds(b * local_blocks, local_blocks)
    far = [
        (d, blk_copy(0, d, lax.rem(b + d, nb_dev), tgt_ref, tgt_all.at[my_blocks]))
        for d in range(2, nb_dev, 2)
    ]
    near = [blk_copy(0, 1, mate, tgt_ref, tgt_all.at[my_blocks])]
    src_copies = to_col(0, lambda peer: src_ref, src_all.at[:, my_rows, :])
    smass_all[c] = jnp.concatenate(
        [smass_ref[...].astype(F32), jnp.zeros((8 - local_blocks, sub), F32)], axis=0)
    masses = tmass_ref[...].astype(F32)
    for q in range(local_blocks):
        tmass_all[b * local_blocks + q] = jnp.broadcast_to(masses[q:q + 1], (8, sub))
    mass_copies = to_col(1, lambda peer: smass_all.at[c], smass_all.at[c])
    mass_copies += to_blk(1, lambda peer: tmass_all.at[my_blocks], tmass_all.at[my_blocks])
    src_all[:, my_rows, :] = src_ref[...]
    tgt_all[my_blocks] = tgt_ref[...]

    total = count_ref[0]
    for p in range(1, local_blocks):
        total = total + count_ref[p]
    for s in range(PAIRS):
        owner, start, end = 0, 0, count_ref[0]
        for p in range(1, local_blocks):
            owner = jnp.where(s >= end, p, owner)
            start = jnp.where(s >= end, end, start)
            end = end + count_ref[p]
        within = jnp.minimum(s - start, slot_max - 1)
        alive = s < total
        slot_src[s] = jnp.int32(owner)
        slot_tgt[s] = jnp.where(alive, home_ref[cand_ref[owner, within]], blocks)
        slot_bias[s] = jnp.where(alive, F32(SHIFT), F32(DEAD))

    @pl.loop(0, blocks)
    def _(n):
        for p in range(local_blocks):
            found = jnp.int32(PAIRS)
            for s in range(PAIRS):
                hit = jnp.logical_and(slot_src[s] == p, slot_tgt[s] == n)
                found = jnp.where(hit, s, found)
            pair_slot[n, p] = found

    back[PAIRS] = jnp.zeros(back.shape[1:], F32)
    for d, copy in far:
        copy.wait_recv()
        came = blocks_of(lax.rem(b - d + nb_dev, nb_dev))
        near.append(blk_copy(3 + ITERS, d, mate, tgt_all.at[came], tgt_all.at[came]))
    finish(near)
    for _, copy in far:
        copy.wait_send()

    @pl.loop(0, PAIRS)
    def _(s):
        tile_unit[s] = unit_rows(tgt_all[jnp.minimum(slot_tgt[s], blocks - 1)].astype(F32))

    row_ids = lax.broadcasted_iota(jnp.int32, (8, full), 0)
    block_ids = lax.broadcasted_iota(jnp.int32, (blocks, sub), 0)
    ones = jnp.where(lax.broadcasted_iota(jnp.int32, (16, sub), 0) < 8, F32(1), F32(0)).astype(BF16)

    def row_part(s, v_rows, running):
        found = lax.dot_general(v_rows, kmat[s], NT, preferred_element_type=F32)
        return running + jnp.where(row_ids == slot_src[s], found[:8] + found[8:], 0.0)

    def score_rows(piece):
        rows = pl.ds(pl.multiple_of(piece * sub, sub), sub)
        for p in range(local_blocks):
            values = src_all[p, rows, :].astype(F32)
            src_unit[p, rows, :] = unit_rows(values)
            src_turned[p, :, rows] = jnp.transpose(values).astype(BF16)
        ids = lax.broadcasted_iota(jnp.int32, (8, sub), 0)

        def one(s, running):
            source = slot_src[s]
            score = lax.dot_general(src_unit[source, rows, :], tile_unit[s], NT,
                                    preferred_element_type=F32)
            tile = jnp.exp2(score * F32(SCALE / width) + slot_bias[s]).astype(BF16)
            kmat[s, rows, :] = tile
            found = lax.dot_general(ones, tile, NT, preferred_element_type=F32)[:8]
            return running + jnp.where(ids == source, found, 0.0)

        row_parts[0, c, :, rows] = lax.fori_loop(0, PAIRS, one, jnp.zeros((8, sub), F32), unroll=2)

    score_rows(c)
    for d in range(1, nc):
        src_copies[d - 1].wait()
        score_rows(lax.rem(c - d + nc, nc))

    def later_step(s, running):
        return row_part(s, v_rep[jnp.minimum(slot_tgt[s], blocks - 1)], running)

    def col_step(s, running):
        found = jnp.dot(u_rep[slot_src[s]], kmat[s], preferred_element_type=F32)
        found = found[:8] + found[8:]
        return running + jnp.where(block_ids == slot_tgt[s], found[:1], 0.0)

    for step in range(ITERS):
        if step > 0:
            row_parts[step, c] = lax.fori_loop(0, PAIRS, later_step, jnp.zeros((8, full), F32), unroll=4)
        finish(to_col(2 + step, lambda peer: row_parts.at[step, c], row_parts.at[step, c]))
        rows = row_parts[step, 0]
        for at in range(1, nc):
            rows = rows + row_parts[step, at]
        rows = jnp.where(row_ids < local_blocks, rows, 1.0)
        row_tot[...] = rows
        if step == 0:
            finish(mass_copies)
        masses = jnp.concatenate([smass_all[at] for at in range(nc)], axis=1)
        scaling_u = masses / rows
        for p in range(local_blocks):
            u_rep[p] = split_rows(scaling_u[p:p + 1])
            if step == ITERS - 1:
                src_turned[p] = (src_turned[p].astype(F32) * scaling_u[p:p + 1]).astype(BF16)
        col_parts[step, b] = lax.fori_loop(0, PAIRS, col_step, jnp.zeros((blocks, sub), F32), unroll=4)
        col_copies = to_blk(2 + step, lambda peer: col_parts.at[step, b], col_parts.at[step, b])
        if step == ITERS - 1:
            @pl.loop(0, PAIRS, unroll=2)
            def _(s):
                back[s] = jnp.dot(src_turned[slot_src[s]], kmat[s], preferred_element_type=F32)

            @pl.loop(0, blocks)
            def _(n):
                piece = back[pair_slot[n, 0]]
                for p in range(1, local_blocks):
                    piece = piece + back[pair_slot[n, p]]
                tgt_send[n] = piece.astype(BF16)

            pair_sums = [
                blk_copy(2 + ITERS, d, mate, tgt_send.at[blocks_of(lax.rem(mate + d, nb_dev))],
                         pair_recv.at[d // 2])
                for d in range(0, nb_dev, 2)
            ]
        finish(col_copies)
        columns = col_parts[step, 0]
        for at in range(1, nb_dev):
            columns = columns + col_parts[step, at]
        col_tot[...] = columns
        @pl.loop(0, blocks)
        def _(n):
            row = tmass_all[n, :1, :] / col_tot[pl.ds(n, 1), :]
            if step < ITERS - 1:
                v_rep[n] = split_rows(row)
            else:
                tgt_all[n] = (tgt_all[n].astype(F32) * column_of(row, width)).astype(BF16)

    def toward_rows(piece):
        rows = pl.ds(pl.multiple_of(piece * sub, sub), sub)
        acc[...] = jnp.zeros(acc.shape, F32)

        @pl.loop(0, PAIRS, unroll=2)
        def _(s):
            tile = tgt_all[jnp.minimum(slot_tgt[s], blocks - 1)]
            toward = jnp.dot(kmat[s, rows, :], tile, preferred_element_type=F32)
            for p in range(local_blocks):
                acc[p] += toward * jnp.where(slot_src[s] == p, F32(1), F32(0))

    src_sums = []
    for d in range(nc - 1, 0, -1):
        peer = lax.rem(c + d, nc)
        toward_rows(peer)
        src_send[d] = acc[...].astype(BF16)
        copy = pltpu.make_async_remote_copy(
            src_ref=src_send.at[d], dst_ref=src_recv.at[d], send_sem=col_ss.at[2 + ITERS, d],
            recv_sem=col_rs.at[2 + ITERS, d], device_id={"col": peer}, device_id_type=MESH)
        copy.start()
        src_sums.append(copy)
    tgt_sums = []
    for d in range(2, nb_dev, 2):
        peer = lax.rem(b + d, nb_dev)
        pair_sums[d // 2].wait_recv()
        pair_send[d // 2] = (tgt_send[blocks_of(peer)].astype(F32)
                             + pair_recv[d // 2].astype(F32)).astype(BF16)
        tgt_sums.append(blk_copy(4 + ITERS, d, peer, pair_send.at[d // 2],
                                 tgt_recv.at[d // 2]))
    pair_sums[0].wait_recv()


    toward_rows(c)
    finish(src_sums)
    for p in range(local_blocks):
        whole = acc[p]
        for at in range(1, nc):
            whole = whole + src_recv[at, p].astype(F32)
        src_out[p] = (whole / column_of(row_tot[p:p + 1, my_rows], width)).astype(BF16)
    finish(tgt_sums)
    for copy in pair_sums:
        copy.wait_send()
    for q in range(local_blocks):
        whole = (tgt_send[b * local_blocks + q].astype(F32) + pair_recv[0, q].astype(F32))
        for at in range(1, nb_dev // 2):
            whole = whole + tgt_recv[at, q].astype(F32)
        whole = whole / col_tot[pl.ds(b * local_blocks + q, 1), :]
        tgt_out[q] = jnp.transpose(whole).astype(BF16)


def local(nb_dev, nc, src_feat, tgt_feat, src_mass, tgt_mass, candidates, counts, tgt_home):
    local_blocks, sub, width = src_feat.shape
    blocks = tgt_home.shape[0]
    full = sub * nc
    vmem = pl.BlockSpec(memory_space=pltpu.VMEM)
    smem = pl.BlockSpec(memory_space=pltpu.SMEM)
    kinds = 3 + ITERS
    shape = jax.ShapeDtypeStruct((local_blocks, sub, width), BF16)
    flops = 2 * PAIRS * full * sub * width * 3
    return pl.pallas_call(
        functools.partial(kernel, nb_dev, nc),
        out_shape=(shape, shape),
        in_specs=[vmem] * 4 + [smem] * 3,
        out_specs=(vmem, vmem),
        scratch_shapes=[
            pltpu.VMEM((local_blocks, full, width), BF16),
            pltpu.VMEM((local_blocks, full, width), BF16),
            pltpu.VMEM((local_blocks, width, full), BF16),
            pltpu.VMEM((blocks, sub, width), BF16),
            pltpu.VMEM((PAIRS, full, sub), BF16),
            pltpu.VMEM((nc, 8, sub), F32),
            pltpu.VMEM((blocks, 8, sub), F32),
            pltpu.VMEM((local_blocks, 16, full), BF16),
            pltpu.VMEM((blocks, 16, sub), BF16),
            pltpu.VMEM((ITERS, nc, 8, full), F32),
            pltpu.VMEM((ITERS, nb_dev, blocks, sub), F32),
            pltpu.VMEM((8, full), F32),
            pltpu.VMEM((blocks, sub), F32),
            pltpu.VMEM((PAIRS + 1, width, sub), F32),
            pltpu.VMEM((local_blocks, sub, width), F32),
            pltpu.VMEM((nc, local_blocks, sub, width), BF16),
            pltpu.VMEM((nc, local_blocks, sub, width), BF16),
            pltpu.VMEM((blocks, width, sub), BF16),
            pltpu.VMEM((nb_dev // 2, local_blocks, width, sub), BF16),
            pltpu.VMEM((nb_dev // 2, local_blocks, width, sub), BF16),
            pltpu.VMEM((nb_dev // 2, local_blocks, width, sub), BF16),
            pltpu.VMEM((PAIRS, sub, width), BF16),
            pltpu.SMEM((PAIRS,), jnp.int32),
            pltpu.SMEM((PAIRS,), jnp.int32),
            pltpu.SMEM((PAIRS,), F32),
            pltpu.SMEM((blocks, local_blocks), jnp.int32),
            pltpu.SemaphoreType.DMA((kinds, nc)),
            pltpu.SemaphoreType.DMA((kinds, nc)),
            pltpu.SemaphoreType.DMA((kinds + 2, nb_dev)),
            pltpu.SemaphoreType.DMA((kinds + 2, nb_dev)),
        ],
        compiler_params=pltpu.CompilerParams(
            collective_id=0, has_side_effects=True, vmem_limit_bytes=56 * 1024 * 1024),
        cost_estimate=pl.CostEstimate(
            flops=flops, bytes_accessed=4 * local_blocks * sub * width * 2,
            transcendentals=PAIRS * full * sub),
    )(src_feat, tgt_feat, src_mass, tgt_mass, candidates, counts, tgt_home)


def solution(mesh):
    in_specs = (
        P("blk", "col", None),
        P("blk", "col", None),
        P("blk", "col"),
        P("blk", "col"),
        P("blk", None),
        P("blk"),
        P(),
    )
    out_specs = (P("blk", "col", None), P("blk", "col", None))
    return jax.shard_map(
        functools.partial(local, mesh.shape["blk"], mesh.shape["col"]),
        mesh=mesh, in_specs=in_specs, out_specs=out_specs, check_vma=False)
```

```python
import functools
import math

import jax
import jax.numpy as jnp
from jax import lax
from jax.experimental import pallas as pl
from jax.experimental.pallas import tpu as pltpu
from jax.sharding import PartitionSpec as P

ITERS = 2
PAIRS = 12
MESH = pl.DeviceIdType.MESH
F32, BF16 = jnp.float32, jnp.bfloat16
LOG2E = math.log2(math.e)
SCALE = LOG2E / 0.02
SHIFT = -0.3 * LOG2E / 0.02
DEAD = -1e30
NT = (((1,), (1,)), ((), ()))


def unit_rows(values):
    inverse = lax.rsqrt(jnp.mean(values * values, axis=-1, keepdims=True) + 1e-6)
    return (values * inverse).astype(BF16)


def split_rows(row):
    wide = jnp.broadcast_to(row, (16, row.shape[1]))
    high = wide.astype(BF16).astype(F32)
    first = lax.broadcasted_iota(jnp.int32, wide.shape, 0) < 8
    return jnp.where(first, high, wide - high).astype(BF16)


def column_of(row, width):
    turned = jnp.transpose(jnp.broadcast_to(row, (128, row.shape[1])))
    return jnp.concatenate([turned] * (width // 128), axis=1)


def kernel(nb_dev, nc, src_ref, tgt_ref, smass_ref, tmass_ref, cand_ref, count_ref, home_ref,
           src_out, tgt_out, src_all, src_unit, src_turned, tgt_all, kmat, smass_all, tmass_all,
           u_rep, v_rep, row_parts, col_parts, row_tot, col_tot, back, acc, src_send, src_recv,
           tgt_send, tgt_recv, pair_send, pair_recv, tile_unit, slot_src, slot_tgt, slot_bias, pair_slot,
           col_ss, col_rs, blk_ss, blk_rs):
    b, c = lax.axis_index("blk"), lax.axis_index("col")
    local_blocks, sub, width = src_ref.shape
    slot_max = cand_ref.shape[1]
    blocks = tgt_all.shape[0]
    full = src_all.shape[1]

    barrier = pltpu.get_barrier_semaphore()
    for d in range(1, nc):
        pl.semaphore_signal(barrier, inc=1, device_id={"col": lax.rem(c + d, nc)}, device_id_type=MESH)
    for d in range(1, nb_dev):
        pl.semaphore_signal(barrier, inc=1, device_id={"blk": lax.rem(b + d, nb_dev)}, device_id_type=MESH)
    pl.semaphore_wait(barrier, nc + nb_dev - 2)

    def to_col(kind, source, target):
        out = []
        for d in range(1, nc):
            peer = lax.rem(c + d, nc)
            copy = pltpu.make_async_remote_copy(
                src_ref=source(peer), dst_ref=target, send_sem=col_ss.at[kind, d],
                recv_sem=col_rs.at[kind, d], device_id={"col": peer}, device_id_type=MESH)
            copy.start()
            out.append(copy)
        return out

    mate = b + 1 - 2 * lax.rem(b, 2)

    def blk_copy(kind, d, peer, source, target):
        copy = pltpu.make_async_remote_copy(
            src_ref=source, dst_ref=target, send_sem=blk_ss.at[kind, d],
            recv_sem=blk_rs.at[kind, d], device_id={"blk": peer}, device_id_type=MESH)
        copy.start()
        return copy

    def blocks_of(index):
        return pl.ds(index * local_blocks, local_blocks)

    def to_blk(kind, source, target):
        out = []
        for d in range(1, nb_dev):
            peer = lax.rem(b + d, nb_dev)
            copy = pltpu.make_async_remote_copy(
                src_ref=source(peer), dst_ref=target, send_sem=blk_ss.at[kind, d],
                recv_sem=blk_rs.at[kind, d], device_id={"blk": peer}, device_id_type=MESH)
            copy.start()
            out.append(copy)
        return out

    def finish(copies):
        for copy in copies:
            copy.wait()

    my_rows = pl.ds(pl.multiple_of(c * sub, sub), sub)
    my_blocks = pl.ds(b * local_blocks, local_blocks)
    far = [
        (d, blk_copy(0, d, lax.rem(b + d, nb_dev), tgt_ref, tgt_all.at[my_blocks]))
        for d in range(2, nb_dev, 2)
    ]
    near = [blk_copy(0, 1, mate, tgt_ref, tgt_all.at[my_blocks])]
    src_copies = to_col(0, lambda peer: src_ref, src_all.at[:, my_rows, :])
    smass_all[c] = jnp.concatenate(
        [smass_ref[...].astype(F32), jnp.zeros((8 - local_blocks, sub), F32)], axis=0)
    masses = tmass_ref[...].astype(F32)
    for q in range(local_blocks):
        tmass_all[b * local_blocks + q] = jnp.broadcast_to(masses[q:q + 1], (8, sub))
    mass_copies = to_col(1, lambda peer: smass_all.at[c], smass_all.at[c])
    mass_copies += to_blk(1, lambda peer: tmass_all.at[my_blocks], tmass_all.at[my_blocks])
    src_all[:, my_rows, :] = src_ref[...]
    tgt_all[my_blocks] = tgt_ref[...]

    total = count_ref[0]
    for p in range(1, local_blocks):
        total = total + count_ref[p]
    for s in range(PAIRS):
        owner, start, end = 0, 0, count_ref[0]
        for p in range(1, local_blocks):
            owner = jnp.where(s >= end, p, owner)
            start = jnp.where(s >= end, end, start)
            end = end + count_ref[p]
        within = jnp.minimum(s - start, slot_max - 1)
        alive = s < total
        slot_src[s] = jnp.int32(owner)
        slot_tgt[s] = jnp.where(alive, home_ref[cand_ref[owner, within]], blocks)
        slot_bias[s] = jnp.where(alive, F32(SHIFT), F32(DEAD))

    @pl.loop(0, blocks)
    def _(n):
        for p in range(local_blocks):
            found = jnp.int32(PAIRS)
            for s in range(PAIRS):
                hit = jnp.logical_and(slot_src[s] == p, slot_tgt[s] == n)
                found = jnp.where(hit, s, found)
            pair_slot[n, p] = found

    back[PAIRS] = jnp.zeros(back.shape[1:], F32)
    for d, copy in far:
        copy.wait_recv()
        came = blocks_of(lax.rem(b - d + nb_dev, nb_dev))
        near.append(blk_copy(3 + ITERS, d, mate, tgt_all.at[came], tgt_all.at[came]))
    finish(near)
    for _, copy in far:
        copy.wait_send()

    @pl.loop(0, PAIRS, unroll=4)
    def _(s):
        tile_unit[s] = unit_rows(tgt_all[jnp.minimum(slot_tgt[s], blocks - 1)].astype(F32))

    row_ids = lax.broadcasted_iota(jnp.int32, (8, full), 0)
    block_ids = lax.broadcasted_iota(jnp.int32, (blocks, sub), 0)
    ones = jnp.where(lax.broadcasted_iota(jnp.int32, (16, sub), 0) < 8, F32(1), F32(0)).astype(BF16)

    def row_part(s, v_rows, running):
        found = lax.dot_general(v_rows, kmat[s], NT, preferred_element_type=F32)
        return running + jnp.where(row_ids == slot_src[s], found[:8] + found[8:], 0.0)

    def score_rows(piece):
        rows = pl.ds(pl.multiple_of(piece * sub, sub), sub)
        for p in range(local_blocks):
            values = src_all[p, rows, :].astype(F32)
            src_unit[p, rows, :] = unit_rows(values)
            src_turned[p, :, rows] = jnp.transpose(values).astype(BF16)
        ids = lax.broadcasted_iota(jnp.int32, (8, sub), 0)

        def one(s, running):
            source = slot_src[s]
            score = lax.dot_general(src_unit[source, rows, :], tile_unit[s], NT,
                                    preferred_element_type=F32)
            tile = jnp.exp2(score * F32(SCALE / width) + slot_bias[s]).astype(BF16)
            kmat[s, rows, :] = tile
            found = lax.dot_general(ones, tile, NT, preferred_element_type=F32)[:8]
            return running + jnp.where(ids == source, found, 0.0)

        row_parts[0, c, :, rows] = lax.fori_loop(0, PAIRS, one, jnp.zeros((8, sub), F32), unroll=6)

    score_rows(c)
    for d in range(1, nc):
        src_copies[d - 1].wait()
        score_rows(lax.rem(c - d + nc, nc))

    def later_step(s, running):
        return row_part(s, v_rep[jnp.minimum(slot_tgt[s], blocks - 1)], running)

    def col_step(s, running):
        found = jnp.dot(u_rep[slot_src[s]], kmat[s], preferred_element_type=F32)
        found = found[:8] + found[8:]
        return running + jnp.where(block_ids == slot_tgt[s], found[:1], 0.0)

    for step in range(ITERS):
        if step > 0:
            row_parts[step, c] = lax.fori_loop(0, PAIRS, later_step, jnp.zeros((8, full), F32), unroll=12)
        finish(to_col(2 + step, lambda peer: row_parts.at[step, c], row_parts.at[step, c]))
        rows = row_parts[step, 0]
        for at in range(1, nc):
            rows = rows + row_parts[step, at]
        rows = jnp.where(row_ids < local_blocks, rows, 1.0)
        row_tot[...] = rows
        if step == 0:
            finish(mass_copies)
        masses = jnp.concatenate([smass_all[at] for at in range(nc)], axis=1)
        scaling_u = masses / rows
        for p in range(local_blocks):
            u_rep[p] = split_rows(scaling_u[p:p + 1])
            if step == ITERS - 1:
                src_turned[p] = (src_turned[p].astype(F32) * scaling_u[p:p + 1]).astype(BF16)
        col_parts[step, b] = lax.fori_loop(0, PAIRS, col_step, jnp.zeros((blocks, sub), F32), unroll=12)
        col_copies = to_blk(2 + step, lambda peer: col_parts.at[step, b], col_parts.at[step, b])
        if step == ITERS - 1:
            @pl.loop(0, PAIRS, unroll=4)
            def _(s):
                back[s] = jnp.dot(src_turned[slot_src[s]], kmat[s], preferred_element_type=F32)

            @pl.loop(0, blocks, unroll=2)
            def _(n):
                piece = back[pair_slot[n, 0]]
                for p in range(1, local_blocks):
                    piece = piece + back[pair_slot[n, p]]
                tgt_send[n] = piece.astype(BF16)

            pair_sums = [
                blk_copy(2 + ITERS, d, mate, tgt_send.at[blocks_of(lax.rem(mate + d, nb_dev))],
                         pair_recv.at[d // 2])
                for d in range(0, nb_dev, 2)
            ]
        finish(col_copies)
        columns = col_parts[step, 0]
        for at in range(1, nb_dev):
            columns = columns + col_parts[step, at]
        col_tot[...] = columns
        @pl.loop(0, blocks, unroll=8)
        def _(n):
            row = tmass_all[n, :1, :] / col_tot[pl.ds(n, 1), :]
            if step < ITERS - 1:
                v_rep[n] = split_rows(row)
            else:
                tgt_all[n] = (tgt_all[n].astype(F32) * column_of(row, width)).astype(BF16)

    def toward_rows(piece):
        rows = pl.ds(pl.multiple_of(piece * sub, sub), sub)
        acc[...] = jnp.zeros(acc.shape, F32)

        @pl.loop(0, PAIRS, unroll=4)
        def _(s):
            tile = tgt_all[jnp.minimum(slot_tgt[s], blocks - 1)]
            toward = jnp.dot(kmat[s, rows, :], tile, preferred_element_type=F32)
            for p in range(local_blocks):
                acc[p] += toward * jnp.where(slot_src[s] == p, F32(1), F32(0))

    src_sums = []
    for d in range(nc - 1, 0, -1):
        peer = lax.rem(c + d, nc)
        toward_rows(peer)
        src_send[d] = acc[...].astype(BF16)
        copy = pltpu.make_async_remote_copy(
            src_ref=src_send.at[d], dst_ref=src_recv.at[d], send_sem=col_ss.at[2 + ITERS, d],
            recv_sem=col_rs.at[2 + ITERS, d], device_id={"col": peer}, device_id_type=MESH)
        copy.start()
        src_sums.append(copy)
    tgt_sums = []
    for d in range(2, nb_dev, 2):
        peer = lax.rem(b + d, nb_dev)
        pair_sums[d // 2].wait_recv()
        pair_send[d // 2] = (tgt_send[blocks_of(peer)].astype(F32)
                             + pair_recv[d // 2].astype(F32)).astype(BF16)
        tgt_sums.append(blk_copy(4 + ITERS, d, peer, pair_send.at[d // 2],
                                 tgt_recv.at[d // 2]))
    pair_sums[0].wait_recv()


    toward_rows(c)
    finish(src_sums)
    for p in range(local_blocks):
        whole = acc[p]
        for at in range(1, nc):
            whole = whole + src_recv[at, p].astype(F32)
        src_out[p] = (whole / column_of(row_tot[p:p + 1, my_rows], width)).astype(BF16)
    finish(tgt_sums)
    for copy in pair_sums:
        copy.wait_send()
    for q in range(local_blocks):
        whole = (tgt_send[b * local_blocks + q].astype(F32) + pair_recv[0, q].astype(F32))
        for at in range(1, nb_dev // 2):
            whole = whole + tgt_recv[at, q].astype(F32)
        whole = whole / col_tot[pl.ds(b * local_blocks + q, 1), :]
        tgt_out[q] = jnp.transpose(whole).astype(BF16)


def local(nb_dev, nc, src_feat, tgt_feat, src_mass, tgt_mass, candidates, counts, tgt_home):
    local_blocks, sub, width = src_feat.shape
    blocks = tgt_home.shape[0]
    full = sub * nc
    vmem = pl.BlockSpec(memory_space=pltpu.VMEM)
    smem = pl.BlockSpec(memory_space=pltpu.SMEM)
    kinds = 3 + ITERS
    shape = jax.ShapeDtypeStruct((local_blocks, sub, width), BF16)
    flops = 2 * PAIRS * full * sub * width * 3
    return pl.pallas_call(
        functools.partial(kernel, nb_dev, nc),
        out_shape=(shape, shape),
        in_specs=[vmem] * 4 + [smem] * 3,
        out_specs=(vmem, vmem),
        scratch_shapes=[
            pltpu.VMEM((local_blocks, full, width), BF16),
            pltpu.VMEM((local_blocks, full, width), BF16),
            pltpu.VMEM((local_blocks, width, full), BF16),
            pltpu.VMEM((blocks, sub, width), BF16),
            pltpu.VMEM((PAIRS, full, sub), BF16),
            pltpu.VMEM((nc, 8, sub), F32),
            pltpu.VMEM((blocks, 8, sub), F32),
            pltpu.VMEM((local_blocks, 16, full), BF16),
            pltpu.VMEM((blocks, 16, sub), BF16),
            pltpu.VMEM((ITERS, nc, 8, full), F32),
            pltpu.VMEM((ITERS, nb_dev, blocks, sub), F32),
            pltpu.VMEM((8, full), F32),
            pltpu.VMEM((blocks, sub), F32),
            pltpu.VMEM((PAIRS + 1, width, sub), F32),
            pltpu.VMEM((local_blocks, sub, width), F32),
            pltpu.VMEM((nc, local_blocks, sub, width), BF16),
            pltpu.VMEM((nc, local_blocks, sub, width), BF16),
            pltpu.VMEM((blocks, width, sub), BF16),
            pltpu.VMEM((nb_dev // 2, local_blocks, width, sub), BF16),
            pltpu.VMEM((nb_dev // 2, local_blocks, width, sub), BF16),
            pltpu.VMEM((nb_dev // 2, local_blocks, width, sub), BF16),
            pltpu.VMEM((PAIRS, sub, width), BF16),
            pltpu.SMEM((PAIRS,), jnp.int32),
            pltpu.SMEM((PAIRS,), jnp.int32),
            pltpu.SMEM((PAIRS,), F32),
            pltpu.SMEM((blocks, local_blocks), jnp.int32),
            pltpu.SemaphoreType.DMA((kinds, nc)),
            pltpu.SemaphoreType.DMA((kinds, nc)),
            pltpu.SemaphoreType.DMA((kinds + 2, nb_dev)),
            pltpu.SemaphoreType.DMA((kinds + 2, nb_dev)),
        ],
        compiler_params=pltpu.CompilerParams(
            collective_id=0, has_side_effects=True, vmem_limit_bytes=56 * 1024 * 1024),
        cost_estimate=pl.CostEstimate(
            flops=flops, bytes_accessed=4 * local_blocks * sub * width * 2,
            transcendentals=PAIRS * full * sub),
    )(src_feat, tgt_feat, src_mass, tgt_mass, candidates, counts, tgt_home)


def solution(mesh):
    in_specs = (
        P("blk", "col", None),
        P("blk", "col", None),
        P("blk", "col"),
        P("blk", "col"),
        P("blk", None),
        P("blk"),
        P(),
    )
    out_specs = (P("blk", "col", None), P("blk", "col", None))
    return jax.shard_map(
        functools.partial(local, mesh.shape["blk"], mesh.shape["col"]),
        mesh=mesh, in_specs=in_specs, out_specs=out_specs, check_vma=False)
```
